1024 devices in a mesh: dp: 256 (over z, x, y_hi), tensor: 4 (over y_lo, core).
Axes of the slice: x: 8, y: 8 (y_hi: 4, y_lo: 2; y = y_hi * 2 + y_lo), z: 8, core: 2. Of those that a mesh axis runs over, the one named last changes fastest.
Arguments:
- picture_averaged_vectors: bfloat16 [49152, 1152], P('dp'), may hold values from -6 to 6
- picture_mapping_matrix: bfloat16 [1152, 1152], P(None, 'tensor'), may hold values from -0.1875 to 0.1875
- caption_averaged_vectors: bfloat16 [49152, 1152], P('dp'), may hold values from -6 to 6
- caption_mapping_matrix: bfloat16 [1152, 1152], P(None, 'tensor'), may hold values from -0.1875 to 0.1875
- sharpness_factor: float32 [1], replicated, may hold values from 3 to 8
- offset_term: float32 [1], replicated, may hold values from -4 to -1
- paired_caption_index: int32 [49152], P('dp'), may hold values from 0 to 49151, as said below
Outputs:
- img_grad: float32 [49152, 1152], P('dp', 'tensor')
- txt_grad: float32 [49152, 1152], P('dp', 'tensor')
The draws below stay inside these ranges and needn't reach their ends.
Inputs may be any that keep to these rules, and one draw needn't show every extreme that they name: paired_caption_index[i] lies in the same aligned block of 192 rows as i, and each text is matched by exactly one image.
All inputs are finite; a program needn't handle non-finite values.
Results may differ from the reference program's by a relative error of at most 0.0041.
Values may be sent and summed in bfloat16 or wider, within the bound.
No kernel may reach another device: no remote copies, remote signals or barrier semaphores. Data moves between devices by JAX's collectives and lax.ppermute only.
A program may use at most 32 MiB of HBM per device.

```python
import jax
import jax.numpy as jnp
from jax import lax

D = 1152
E = 1152
B_DEV = 192
SPAN = 8
B = 49152
N_DP = 256


def draw_paired_caption_index(key, part):
    key = jax.random.fold_in(key, 5)
    blocks = B // B_DEV
    keys = jax.random.split(key, blocks)
    perms = jax.vmap(lambda k: jax.random.permutation(k, B_DEV))(keys)
    offsets = jnp.arange(blocks, dtype=jnp.int32)[:, None] * B_DEV
    return (perms.astype(jnp.int32) + offsets).reshape(-1).astype(jnp.int32)


def block_scale(key, extent, shards, least, largest):
    loudness, own = 1.0, jax.random.fold_in(key, 6)
    for position, parts in shards:
        draws = jnp.exp(jax.random.uniform(jax.random.fold_in(own, position), (parts,), jnp.float32, least / len(shards), largest / len(shards)))
        loudness = loudness * jnp.repeat(draws, extent[position] // parts).reshape([-1 if axis == position else 1 for axis in range(len(extent))])
    return loudness


def gaussian(own_key, shape, spread, reach, cuts=(), kind=jnp.bfloat16):
    result = jax.random.normal(own_key, shape, jnp.float32) * spread
    if len(cuts) > 0:
        result = block_scale(own_key, shape, cuts, -0.22, 0.18) * result
    return jnp.clip(result, min=-reach, max=reach).astype(kind)


def setup_inputs(seed: int = 0) -> dict:
    arg_keys = jax.random.split(jax.random.key(seed), 8)
    picture_averaged_vectors = gaussian(arg_keys[0], (B, D), 1.0, 6.0, ((0, 256),))
    picture_mapping_matrix = gaussian(arg_keys[1], (D, E), D ** -0.5, 0.1875, ((1, 4),))
    caption_averaged_vectors = gaussian(arg_keys[2], (B, D), 1.0, 6.0, ((0, 256),))
    caption_mapping_matrix = gaussian(arg_keys[3], (D, E), D ** -0.5, 0.1875, ((1, 4),))
    sharpness_factor = jnp.clip(jax.random.uniform(arg_keys[4], (1,), jnp.float32, 3.0, 8.0), 3.0, 8.0)
    offset_term = jnp.clip(jax.random.uniform(arg_keys[5], (1,), jnp.float32, -4.0, -1.0), -4.0, -1.0)
    paired_caption_index = draw_paired_caption_index(jax.random.fold_in(arg_keys[7], 71), 0)
    return dict(picture_averaged_vectors=picture_averaged_vectors, picture_mapping_matrix=picture_mapping_matrix, caption_averaged_vectors=caption_averaged_vectors, caption_mapping_matrix=caption_mapping_matrix, sharpness_factor=sharpness_factor, offset_term=offset_term, paired_caption_index=paired_caption_index)


def unit_rows(emb):
    inv = lax.rsqrt(lax.optimization_barrier(jnp.sum(emb * emb, axis=1)) + 1e-06)
    return (inv, emb * inv[:, None])

def back_norm(inv, unit, dunit):
    inner = lax.optimization_barrier(jnp.sum(unit * dunit, axis=1))
    return inv[:, None] * (dunit - unit * inner[:, None])

def reference(picture_averaged_vectors, picture_mapping_matrix, caption_averaged_vectors, caption_mapping_matrix, sharpness_factor, offset_term, paired_caption_index):
    img_emb = jnp.dot(picture_averaged_vectors, picture_mapping_matrix, preferred_element_type=jnp.float32)
    txt_emb = jnp.dot(caption_averaged_vectors, caption_mapping_matrix, preferred_element_type=jnp.float32)
    inv_img, img_unit = unit_rows(img_emb)
    inv_txt, txt_unit = unit_rows(txt_emb)
    img_low = img_unit.astype(jnp.bfloat16)
    txt_low = txt_unit.astype(jnp.bfloat16)
    similarity_multiplier = sharpness_factor[0]
    width = img_low.shape[1]
    img_blocks = img_low.astype(jnp.float32).reshape(N_DP, B_DEV, width)
    txt_blocks = txt_low.astype(jnp.float32).reshape(N_DP, B_DEV, width)
    matching_text_blocks = paired_caption_index.reshape(N_DP, B_DEV)
    own_ids = jnp.arange(N_DP, dtype=jnp.int32)[:, None] * B_DEV + jnp.arange(B_DEV, dtype=jnp.int32)[None, :]
    own_sign = jnp.where(matching_text_blocks[:, :, None] == own_ids[:, None, :], 1.0, -1.0).astype(jnp.float32)
    image_partial_sum = jnp.zeros((N_DP, B_DEV, width), jnp.float32)
    txt_sum = jnp.zeros((N_DP, B_DEV, width), jnp.float32)
    for step in range(SPAN):
        rolled = jnp.roll(txt_blocks, -step, axis=0)
        logits = similarity_multiplier * jnp.einsum('nbe,nce->nbc', img_blocks, rolled) + offset_term[0]
        if step == 0:
            sign = own_sign
        else:
            sign = -jnp.ones_like(logits)
        weight = (-16.0 * sign * jax.nn.sigmoid(-sign * logits)).astype(jnp.bfloat16).astype(jnp.float32)
        image_partial_sum = image_partial_sum + jnp.einsum('nbc,nce->nbe', weight, rolled)
        txt_sum = txt_sum + jnp.roll(jnp.einsum('nbc,nbe->nce', weight, img_blocks), step, axis=0)
    img_dunit = similarity_multiplier * image_partial_sum.reshape(-1, width)
    txt_dunit = similarity_multiplier * txt_sum.reshape(-1, width)
    img_demb = back_norm(inv_img, img_unit, img_dunit)
    txt_demb = back_norm(inv_txt, txt_unit, txt_dunit)
    img_grad = jnp.dot(img_demb, picture_mapping_matrix.astype(jnp.float32).T, precision=lax.Precision.HIGHEST)
    txt_grad = jnp.dot(txt_demb, caption_mapping_matrix.astype(jnp.float32).T, precision=lax.Precision.HIGHEST)
    return (img_grad, txt_grad)
```

```python
import jax
import jax.numpy as jnp
from jax import lax
from jax.sharding import PartitionSpec as P

AXES = ("dp", "tensor")
ROUND = 4


def exchange(block, groups, source):
    route = []
    for n in range(groups):
        for t in range(4):
            m, u = source(n, t)
            route.append(((m % groups) * 4 + u, n * 4 + t))
    return lax.ppermute(block, AXES, route)


def neighbour(n, t):
    return [(n + 3, 2), (n - 1, 3), (n + 1, 0), (n - 3, 1)][t]


def relay(n, t):
    return (n - 1, t) if t < 2 else (n + 1, t)


def beyond(n, t):
    return (n + ROUND, t) if t % 2 == 0 else (n - ROUND, t)


def chip_swap(n, t):
    return (n, t ^ 2)


def core_swap(n, t):
    return (n, t ^ 1)


def shards(
    picture_averaged_vectors,
    picture_mapping_matrix,
    caption_averaged_vectors,
    caption_mapping_matrix,
    sharpness_factor,
    offset_term,
    paired_caption_index,
):
    f32, bf16 = jnp.float32, jnp.bfloat16
    groups = lax.axis_size("dp")
    rows = picture_averaged_vectors.shape[0]
    half = rows // 2
    span = picture_mapping_matrix.shape[1]
    scale = sharpness_factor[0]
    offset = offset_term[0]
    t = lax.axis_index("tensor")
    core0 = t % 2 == 0
    chip0 = t < 2

    img_emb = jnp.dot(
        picture_averaged_vectors, picture_mapping_matrix, preferred_element_type=f32
    )
    txt_emb = jnp.dot(
        caption_averaged_vectors, caption_mapping_matrix, preferred_element_type=f32
    )
    squares = jnp.concatenate(
        [jnp.sum(img_emb * img_emb, axis=1), jnp.sum(txt_emb * txt_emb, axis=1)]
    )
    inv = lax.rsqrt(lax.psum(squares, "tensor") + 1e-06)
    inv_img, inv_txt = inv[:rows], inv[rows:]
    img_unit = img_emb * inv_img[:, None]
    txt_unit = txt_emb * inv_txt[:, None]
    img_low = img_unit.astype(bf16)
    txt_low = txt_unit.astype(bf16)
    img_rest = (img_unit - img_low.astype(f32)).astype(bf16)
    txt_rest = (txt_unit - txt_low.astype(f32)).astype(bf16)

    def by_core(a, b):
        return jnp.where(core0, a, b), jnp.where(core0, b, a)

    def by_chip(mine, other):
        return jnp.where(chip0, mine, other), jnp.where(chip0, other, mine)

    fixed_part, moving_part = by_core(img_low, txt_low)
    own = jnp.concatenate([fixed_part, moving_part])
    other = exchange(own, groups, chip_swap)
    first, second = by_chip(own, other)
    pair = jnp.concatenate([first, second], axis=1)
    peer = exchange(pair, groups, core_swap)

    def whole(mine, theirs):
        return jnp.concatenate(
            [mine[:, :span], theirs[:, :span], mine[:, span:], theirs[:, span:]], axis=1
        )

    fixed = whole(pair[:rows], peer[rows:])
    moving = whole(pair[rows:], peer[:rows])
    own_half = jnp.where(chip0, moving[:half], moving[half:])

    near = exchange(moving, groups, neighbour)
    far_own = exchange(own_half, groups, beyond)

    rest_mine, rest_theirs = by_core(img_rest, txt_rest)
    rest_peer = exchange(rest_theirs, groups, core_swap)
    rest_chip = jnp.concatenate([rest_mine, rest_peer], axis=1)
    rest_other = exchange(rest_chip, groups, chip_swap)
    rest = jnp.concatenate(by_chip(rest_chip, rest_other), axis=1)
    matrix_mine, matrix_theirs = by_core(picture_mapping_matrix, caption_mapping_matrix)
    matrix_peer = exchange(matrix_theirs, groups, core_swap)

    near_half = jnp.where(chip0, near[:half], near[half:])
    opposite = exchange(near_half, groups, relay)
    far_near = exchange(near, groups, beyond)
    far_opposite = exchange(opposite, groups, beyond)

    def products(block):
        return scale * lax.dot_general(
            fixed, block, (((1,), (1,)), ((), ())), preferred_element_type=f32
        ) + offset

    def pull(weight, block):
        return jnp.dot(weight.astype(bf16), block, preferred_element_type=f32)

    def unmatched(block):
        return pull(16.0 * jax.nn.sigmoid(products(block)), block)

    first_row = lax.axis_index("dp") * rows
    ids = first_row + jnp.arange(rows, dtype=jnp.int32)
    half_ids = jnp.where(chip0, ids[:half], ids[half:])
    half_index = jnp.where(chip0, paired_caption_index[:half], paired_caption_index[half:])
    matched = jnp.where(
        core0,
        paired_caption_index[:, None] == half_ids[None, :],
        ids[:, None] == half_index[None, :],
    )
    sign = jnp.where(matched, 1.0, -1.0).astype(f32)
    total = pull(-16.0 * sign * jax.nn.sigmoid(-sign * products(own_half)), own_half)
    total = total + unmatched(far_own)
    total = total + unmatched(near)
    total = total + unmatched(opposite)
    total = total + unmatched(far_near)
    total = total + unmatched(far_opposite)

    unit = fixed.astype(f32) + rest.astype(f32)
    across = total - unit * jnp.sum(unit * total, axis=1, keepdims=True)
    keep, give = by_chip(across[:, : 2 * span], across[:, 2 * span :])
    got = exchange(give.astype(bf16), groups, chip_swap)
    inv_fixed = jnp.where(core0, inv_img, inv_txt)
    demb = (scale * inv_fixed)[:, None] * (keep + got.astype(f32))
    demb_high = demb.astype(bf16)
    demb_rest = (demb - demb_high.astype(f32)).astype(bf16)
    matrix = jnp.concatenate([matrix_mine, matrix_peer], axis=1)
    by_columns = (((1,), (1,)), ((), ()))
    part = lax.dot_general(
        demb_high, matrix, by_columns, preferred_element_type=f32
    ) + lax.dot_general(demb_rest, matrix, by_columns, preferred_element_type=f32)
    keep, give = by_chip(part[:, : 2 * span], part[:, 2 * span :])
    got = exchange(give.astype(bf16), groups, chip_swap)
    grad = keep + got.astype(f32)
    mine, theirs = by_core(grad[:, :span], grad[:, span:])
    peer_grad = exchange(theirs, groups, core_swap)
    return by_core(mine, peer_grad)


def solution(mesh):
    in_specs = (
        P("dp", None),
        P(None, "tensor"),
        P("dp", None),
        P(None, "tensor"),
        P(),
        P(),
        P("dp"),
    )
    out_specs = (P("dp", "tensor"), P("dp", "tensor"))
    return jax.shard_map(shards, mesh=mesh, in_specs=in_specs, out_specs=out_specs, check_vma=False)
```

```python
import jax
import jax.numpy as jnp
from jax import lax
from jax.experimental import pallas as pl
from jax.experimental.pallas import tpu as pltpu
from jax.sharding import PartitionSpec as P

AXES = ("dp", "tensor")
ROUND = 4
LANES = 128
F32, BF16 = jnp.float32, jnp.bfloat16
BY_COLUMNS = (((1,), (1,)), ((), ()))


def exchange(block, groups, source):
    route = []
    for n in range(groups):
        for t in range(4):
            m, u = source(n, t)
            route.append(((m % groups) * 4 + u, n * 4 + t))
    return lax.ppermute(block, AXES, route)


def neighbour(n, t):
    return [(n + 3, 2), (n - 1, 3), (n + 1, 0), (n - 3, 1)][t]


def relay(n, t):
    return (n - 1, t) if t < 2 else (n + 1, t)


def beyond(n, t):
    return (n + ROUND, t) if t % 2 == 0 else (n - ROUND, t)


def chip_swap(n, t):
    return (n, t ^ 2)


def core_swap(n, t):
    return (n, t ^ 1)


def cross_swap(n, t):
    return (n, t ^ 3)


def call(kernel, outs, *operands, scratch=(), flops=0):
    specs = [
        pl.BlockSpec(memory_space=pltpu.SMEM if x.ndim == 1 else pltpu.VMEM) for x in operands
    ]
    moved = sum(x.size * x.dtype.itemsize for x in operands)
    return pl.pallas_call(
        kernel,
        cost_estimate=pl.CostEstimate(flops=flops, bytes_accessed=moved, transcendentals=0),
        out_shape=[jax.ShapeDtypeStruct(shape, dtype) for shape, dtype in outs],
        in_specs=specs,
        out_specs=[pl.BlockSpec(memory_space=pltpu.VMEM)] * len(outs),
        scratch_shapes=[pltpu.VMEM(shape, dtype) for shape, dtype in scratch],
        compiler_params=pltpu.CompilerParams(vmem_limit_bytes=24 * 2**20),
    )(*operands)


def packed_rows(rows, columns):
    whole, rest = columns // LANES, columns % LANES
    return rows * whole + (rows * rest) // LANES


def pack(ref, at, value):
    rows, columns = value.shape
    whole, rest = columns // LANES, columns % LANES
    for i in range(whole):
        ref[at + i * rows : at + (i + 1) * rows, :] = value[:, i * LANES : (i + 1) * LANES]
    if rest:
        side = LANES // rest
        short = rows // side
        at = at + whole * rows
        ref[at : at + short, :] = jnp.concatenate(
            [value[i * short : (i + 1) * short, whole * LANES :] for i in range(side)], axis=1
        )


def unpack(ref, at, rows, columns):
    whole, rest = columns // LANES, columns % LANES
    tiles = [ref[at + i * rows : at + (i + 1) * rows, :] for i in range(whole)]
    if rest:
        side = LANES // rest
        short = rows // side
        last = ref[at + whole * rows : at + whole * rows + short, :]
        tiles.append(
            jnp.concatenate([last[:, i * rest : (i + 1) * rest] for i in range(side)], axis=0)
        )
    return jnp.concatenate(tiles, axis=1)


def beside(parts, axis):
    cut = parts[0].shape[axis] // LANES * LANES
    size = parts[0].shape[axis]
    return jnp.concatenate(
        [lax.slice_in_dim(x, 0, cut, axis=axis) for x in parts]
        + [lax.slice_in_dim(x, cut, size, axis=axis) for x in parts],
        axis=axis,
    )


def unit_parts(place, img, txt, own, fixed, moving, rest_mine, rest_theirs):
    rows, span = img.shape
    core0 = place[0] == 0
    a, b = img[...], txt[...]
    keep, travel = jnp.where(core0, a, b), jnp.where(core0, b, a)
    keep_low, travel_low = keep.astype(BF16), travel.astype(BF16)
    fixed[...] = keep_low
    moving[...] = travel_low
    rest_mine[...] = (keep - keep_low.astype(F32)).astype(BF16)
    rest_theirs[...] = (travel - travel_low.astype(F32)).astype(BF16)
    pack(own, 0, keep_low)
    pack(own, packed_rows(rows, span), travel_low)


def pair_up(place, fixed, moving, got, pair):
    rows, span = fixed.shape
    chip0 = place[1] == 0
    second = packed_rows(rows, span)
    for i, ref in enumerate((fixed, moving)):
        own, other = ref[...], unpack(got, i * second, rows, span)
        first, last = jnp.where(chip0, own, other), jnp.where(chip0, other, own)
        pair[i * rows : (i + 1) * rows, :] = beside([first, last], 1)


def whole_width(place, pair, peer, fixed, own_half, other_half):
    rows = fixed.shape[0]
    half = rows // 2
    span = pair.shape[1] // 2
    cut = span // LANES * LANES
    chip0 = place[1] == 0

    def widened(i):
        mine = pair[i * rows : (i + 1) * rows, :]
        theirs = peer[(1 - i) * rows : (2 - i) * rows, :]
        end = cut + span
        return jnp.concatenate(
            [mine[:, :cut], theirs[:, :cut], mine[:, cut : 2 * cut], theirs[:, cut : 2 * cut]]
            + [mine[:, 2 * cut : end], theirs[:, 2 * cut : end], mine[:, end:], theirs[:, end:]],
            axis=1,
        )

    fixed[...] = widened(0)
    moving = widened(1)
    top, bottom = moving[:half], moving[half:]
    own_half[...] = jnp.where(chip0, top, bottom)
    other_half[...] = jnp.where(chip0, bottom, top)


def pull(factors, fixed, block, sign=None):
    logits = factors[0] * lax.dot_general(
        fixed, block, BY_COLUMNS, preferred_element_type=F32
    ) + factors[1]
    if sign is None:
        weight = 16.0 * jax.nn.sigmoid(logits)
    else:
        weight = -16.0 * sign * jax.nn.sigmoid(-sign * logits)
    return jnp.dot(weight.astype(BF16), block, preferred_element_type=F32)


def first_sum(factors, fixed, sign, own_half, total):
    total[...] = pull(factors, fixed[...], own_half[...], sign[...])


def next_sum(factors, fixed, before, *refs):
    block = jnp.concatenate([x[...] for x in refs[:-1]], axis=0)
    refs[-1][...] = before[...] + pull(factors, fixed[...], block)


def on_diagonal(rows):
    shape = (rows, rows)
    return lax.broadcasted_iota(jnp.int32, shape, 0) == lax.broadcasted_iota(jnp.int32, shape, 1)


def last_sum(place, factors, fixed, before, far_opposite, inv, keep, inner_kept, give):
    rows, width = fixed.shape
    span = width // 4
    cut = span // LANES * LANES
    chip0 = place[1] == 0
    a = fixed[...]
    total = before[...] + pull(factors, a, far_opposite[...])
    unit = a.astype(F32)
    by_row = factors[0] * inv[...]
    inner = jnp.sum(unit * total, axis=1, keepdims=True) * by_row
    across = total * by_row - unit * inner
    middle = 4 * cut + 2 * (span - cut)
    first = jnp.concatenate([across[:, : 2 * cut], across[:, 4 * cut : middle]], axis=1)
    last = jnp.concatenate([across[:, 2 * cut : 4 * cut], across[:, middle:]], axis=1)
    keep[...] = jnp.where(chip0, first, last)
    inner_kept[...] = inner
    pack(give, 0, jnp.where(chip0, last, first).astype(BF16))
    at = packed_rows(rows, 2 * span)
    line = jnp.sum(jnp.where(on_diagonal(rows), inner, 0.0), axis=0, keepdims=True)
    give[at : at + 16, :] = jnp.broadcast_to(line[:, :LANES], (16, LANES)).astype(BF16)
    give[at + 16 : at + 32, :] = jnp.broadcast_to(line[:, rows - LANES :], (16, LANES)).astype(BF16)


def finish_sum(kept, inner_kept, got, rest_mine, rest_peer, stacked):
    rows, width = kept.shape
    at = packed_rows(rows, width)
    start, end = got[at : at + 1, :], got[at + 16 : at + 17, :]
    line = jnp.concatenate([start, end[:, 2 * LANES - rows :]], axis=1).astype(F32)
    other = jnp.sum(jnp.where(on_diagonal(rows), line, 0.0), axis=1, keepdims=True)
    rest = beside([rest_mine[...], rest_peer[...]], 1).astype(F32)
    demb = kept[...] + unpack(got, 0, rows, width).astype(F32) - rest * (inner_kept[...] + other)
    high = demb.astype(BF16)
    stacked[:rows, :] = high
    stacked[rows:, :] = (demb - high.astype(F32)).astype(BF16)


def through_matrix(
    place, kept, inner_kept, got, rest_mine, rest_peer, mine, peer, to_chip, to_cross, to_core, keep, stacked
):
    rows, width = kept.shape
    span = width // 2
    finish_sum(kept, inner_kept, got, rest_mine, rest_peer, stacked)
    matrix = beside([mine[...], peer[...]], 0)
    part = jnp.dot(stacked[...], matrix, preferred_element_type=F32)
    part = part[:rows] + part[rows:]
    spans = [part[:, u * span : (u + 1) * span] for u in range(4)]
    for t in range(4):

        @pl.when(2 * place[1] + place[0] == t)
        def _(t=t):
            pack(to_chip, 0, spans[t ^ 2].astype(BF16))
            pack(to_cross, 0, spans[t ^ 3].astype(BF16))
            pack(to_core, 0, spans[t ^ 1].astype(BF16))
            keep[...] = spans[t]


def last_add(place, from_chip, from_cross, from_core, kept, img, txt):
    rows, span = kept.shape
    core0 = place[0] == 0
    mine = kept[...] + unpack(from_chip, 0, rows, span).astype(F32)
    theirs = unpack(from_core, 0, rows, span).astype(F32)
    theirs = theirs + unpack(from_cross, 0, rows, span).astype(F32)
    img[...] = jnp.where(core0, mine, theirs)
    txt[...] = jnp.where(core0, theirs, mine)


def shards(
    picture_averaged_vectors,
    picture_mapping_matrix,
    caption_averaged_vectors,
    caption_mapping_matrix,
    sharpness_factor,
    offset_term,
    paired_caption_index,
):
    groups = lax.axis_size("dp")
    rows = picture_averaged_vectors.shape[0]
    half = rows // 2
    span = picture_mapping_matrix.shape[1]
    width = 4 * span
    t = lax.axis_index("tensor")
    core0 = t % 2 == 0
    chip0 = t < 2
    place = jnp.stack([t % 2, t // 2]).astype(jnp.int32)
    factors = jnp.concatenate([sharpness_factor, offset_term])

    img_emb = jnp.dot(
        picture_averaged_vectors, picture_mapping_matrix, preferred_element_type=F32
    )
    txt_emb = jnp.dot(
        caption_averaged_vectors, caption_mapping_matrix, preferred_element_type=F32
    )
    squares = jnp.concatenate(
        [jnp.sum(img_emb * img_emb, axis=1), jnp.sum(txt_emb * txt_emb, axis=1)]
    )
    inv = lax.rsqrt(lax.psum(squares, "tensor") + 1e-06)
    inv_img, inv_txt = inv[:rows], inv[rows:]
    img_unit = img_emb * inv_img[:, None]
    txt_unit = txt_emb * inv_txt[:, None]
    piece = ((rows, span), BF16)
    own, fixed_own, moving_own, rest_mine, rest_theirs = call(
        unit_parts,
        [((2 * packed_rows(rows, span), LANES), BF16)] + [piece] * 4,
        place,
        img_unit,
        txt_unit,
    )
    other = exchange(own, groups, chip_swap)
    rest_peer = exchange(rest_theirs, groups, core_swap)
    img_matrix, txt_matrix, _ = lax.optimization_barrier(
        (picture_mapping_matrix.T, caption_mapping_matrix.T, own)
    )
    matrix_mine = jnp.where(core0, img_matrix, txt_matrix)
    matrix_theirs = jnp.where(core0, txt_matrix, img_matrix)
    matrix_peer = exchange(matrix_theirs, groups, core_swap)
    (pair,) = call(pair_up, [((2 * rows, 2 * span), BF16)], place, fixed_own, moving_own, other)
    peer = exchange(pair, groups, core_swap)
    peer, matrix_peer = lax.optimization_barrier((peer, matrix_peer))
    fixed, own_half, other_half = call(
        whole_width,
        [((rows, width), BF16), ((half, width), BF16), ((half, width), BF16)],
        place,
        pair,
        peer,
    )

    inv_fixed = jnp.where(core0, inv_img, inv_txt)[:, None]

    first_row = lax.axis_index("dp") * rows
    ids = first_row + jnp.arange(rows, dtype=jnp.int32)
    half_ids = jnp.where(chip0, ids[:half], ids[half:])
    half_index = jnp.where(chip0, paired_caption_index[:half], paired_caption_index[half:])
    matched = jnp.where(
        core0,
        paired_caption_index[:, None] == half_ids[None, :],
        ids[:, None] == half_index[None, :],
    )
    sign = jnp.where(matched, 1.0, -1.0).astype(F32)

    sums = [((rows, width), F32)]
    near_relayed = exchange(other_half, groups, neighbour)
    near_other = exchange(own_half, groups, neighbour)
    (total,) = call(first_sum, sums, factors, fixed, sign, own_half)
    near_relayed, total = lax.optimization_barrier((near_relayed, total))
    opposite = exchange(near_relayed, groups, relay)
    far_own = exchange(own_half, groups, beyond)
    far_relayed = exchange(near_relayed, groups, beyond)
    far_other = exchange(near_other, groups, beyond)
    far_opposite = exchange(opposite, groups, beyond)
    nearer = (near_relayed, near_other, opposite)
    (total,) = call(
        next_sum, sums, factors, fixed, total, *nearer, far_own, far_relayed, far_other
    )
    keep, inner_kept, give = call(
        last_sum,
        [
            ((rows, 2 * span), F32),
            ((rows, 1), F32),
            ((packed_rows(rows, 2 * span) + 32, LANES), BF16),
        ],
        place,
        factors,
        fixed,
        total,
        far_opposite,
        inv_fixed,
    )
    got = exchange(give, groups, chip_swap)
    part = ((rows, span), F32)
    sent = ((packed_rows(rows, span), LANES), BF16)
    to_chip, to_cross, to_core, keep = call(
        through_matrix,
        [sent, sent, sent, part],
        place,
        keep,
        inner_kept,
        got,
        rest_mine,
        rest_peer,
        matrix_mine,
        matrix_peer,
        scratch=[((2 * rows, 2 * span), BF16)],
    )
    from_chip = exchange(to_chip, groups, chip_swap)
    from_cross = exchange(to_cross, groups, cross_swap)
    from_core = exchange(to_core, groups, core_swap)
    return tuple(call(last_add, [part, part], place, from_chip, from_cross, from_core, keep))


def solution(mesh):
    in_specs = (
        P("dp", None),
        P(None, "tensor"),
        P("dp", None),
        P(None, "tensor"),
        P(),
        P(),
        P("dp"),
    )
    out_specs = (P("dp", "tensor"), P("dp", "tensor"))
    return jax.shard_map(shards, mesh=mesh, in_specs=in_specs, out_specs=out_specs, check_vma=False)
```

```python
import jax
import jax.numpy as jnp
from jax import lax
from jax.experimental import pallas as pl
from jax.experimental.pallas import tpu as pltpu
from jax.sharding import PartitionSpec as P

AXES = ("dp", "tensor")
ROUND = 4
LANES = 128
F32, BF16 = jnp.float32, jnp.bfloat16
BY_COLUMNS = (((1,), (1,)), ((), ()))


def exchange(block, groups, source):
    route = []
    for n in range(groups):
        for t in range(4):
            m, u = source(n, t)
            route.append(((m % groups) * 4 + u, n * 4 + t))
    return lax.ppermute(block, AXES, route)


def neighbour(n, t):
    return [(n + 3, 2), (n - 1, 3), (n + 1, 0), (n - 3, 1)][t]


def relay(n, t):
    return (n - 1, t) if t < 2 else (n + 1, t)


def beyond(n, t):
    return (n + ROUND, t) if t % 2 == 0 else (n - ROUND, t)


def chip_swap(n, t):
    return (n, t ^ 2)


def core_swap(n, t):
    return (n, t ^ 1)


def cross_swap(n, t):
    return (n, t ^ 3)


def position():
    t = lax.axis_index("tensor")
    return lax.rem(t, 2), lax.div(t, 2)


def call(kernel, outs, *operands, scratch=(), flops=0):
    specs = [
        pl.BlockSpec(memory_space=pltpu.SMEM if x.ndim == 1 else pltpu.VMEM) for x in operands
    ]
    moved = sum(x.size * x.dtype.itemsize for x in operands)
    return pl.pallas_call(
        kernel,
        cost_estimate=pl.CostEstimate(flops=flops, bytes_accessed=moved, transcendentals=0),
        out_shape=[jax.ShapeDtypeStruct(shape, dtype) for shape, dtype in outs],
        in_specs=specs,
        out_specs=[pl.BlockSpec(memory_space=pltpu.VMEM)] * len(outs),
        scratch_shapes=[pltpu.VMEM(shape, dtype) for shape, dtype in scratch],
        compiler_params=pltpu.CompilerParams(vmem_limit_bytes=24 * 2**20),
    )(*operands)


def packed_rows(rows, columns):
    whole, rest = columns // LANES, columns % LANES
    return rows * whole + (rows * rest) // LANES


def pack(ref, at, value):
    rows, columns = value.shape
    whole, rest = columns // LANES, columns % LANES
    for i in range(whole):
        ref[at + i * rows : at + (i + 1) * rows, :] = value[:, i * LANES : (i + 1) * LANES]
    if rest:
        side = LANES // rest
        short = rows // side
        at = at + whole * rows
        ref[at : at + short, :] = jnp.concatenate(
            [value[i * short : (i + 1) * short, whole * LANES :] for i in range(side)], axis=1
        )


def unpack(ref, at, rows, columns):
    whole, rest = columns // LANES, columns % LANES
    tiles = [ref[at + i * rows : at + (i + 1) * rows, :] for i in range(whole)]
    if rest:
        side = LANES // rest
        short = rows // side
        last = ref[at + whole * rows : at + whole * rows + short, :]
        tiles.append(
            jnp.concatenate([last[:, i * rest : (i + 1) * rest] for i in range(side)], axis=0)
        )
    return jnp.concatenate(tiles, axis=1)


def beside(parts, axis):
    cut = parts[0].shape[axis] // LANES * LANES
    size = parts[0].shape[axis]
    return jnp.concatenate(
        [lax.slice_in_dim(x, 0, cut, axis=axis) for x in parts]
        + [lax.slice_in_dim(x, cut, size, axis=axis) for x in parts],
        axis=axis,
    )


def unit_parts(img, txt, own, fixed, moving, rest_mine, rest_theirs):
    core, chip = position()
    rows, span = img.shape
    core0 = core == 0
    a, b = img[...], txt[...]
    keep, travel = jnp.where(core0, a, b), jnp.where(core0, b, a)
    keep_low, travel_low = keep.astype(BF16), travel.astype(BF16)
    fixed[...] = keep_low
    moving[...] = travel_low
    rest_mine[...] = (keep - keep_low.astype(F32)).astype(BF16)
    rest_theirs[...] = (travel - travel_low.astype(F32)).astype(BF16)
    pack(own, 0, keep_low)
    pack(own, packed_rows(rows, span), travel_low)


def pair_up(fixed, moving, got, pair):
    core, chip = position()
    rows, span = fixed.shape
    chip0 = chip == 0
    second = packed_rows(rows, span)
    for i, ref in enumerate((fixed, moving)):
        own, other = ref[...], unpack(got, i * second, rows, span)
        first, last = jnp.where(chip0, own, other), jnp.where(chip0, other, own)
        pair[i * rows : (i + 1) * rows, :] = beside([first, last], 1)


def widened(mine, theirs):
    span = mine.shape[1] // 2
    cut = span // LANES * LANES
    end = cut + span
    return jnp.concatenate(
        [mine[:, :cut], theirs[:, :cut], mine[:, cut : 2 * cut], theirs[:, cut : 2 * cut]]
        + [mine[:, 2 * cut : end], theirs[:, 2 * cut : end], mine[:, end:], theirs[:, end:]],
        axis=1,
    )


def wide_half(own, pair, peer, out):
    half = out.shape[0]
    rows = 2 * half
    _, chip = position()
    for first in (True, False):

        @pl.when((chip == 0) == (first == own))
        def _(first=first):
            at = 0 if first else half
            mine, theirs = pair[rows + at : rows + at + half, :], peer[at : at + half, :]
            out[...] = widened(mine, theirs)


def relayed_half(pair, peer, other_half):
    wide_half(False, pair, peer, other_half)


def fixed_and_half(pair, peer, fixed, own_half):
    rows = fixed.shape[0]
    fixed[...] = widened(pair[:rows, :], peer[rows:, :])
    wide_half(True, pair, peer, own_half)


def pull(factors, fixed, block, sign=None):
    logits = factors[0:1, 0:1] * lax.dot_general(
        fixed, block, BY_COLUMNS, preferred_element_type=F32
    ) + factors[1:2, 0:1]
    if sign is None:
        weight = 16.0 * jax.nn.sigmoid(logits)
    else:
        weight = -16.0 * sign * jax.nn.sigmoid(-sign * logits)
    return jnp.dot(weight.astype(BF16), block, preferred_element_type=F32)


def first_sum(factors, fixed, sign, own_half, total):
    total[...] = pull(factors, fixed[...], own_half[...], sign[...])


def next_sum(factors, fixed, before, *refs):
    block = jnp.concatenate([x[...] for x in refs[:-1]], axis=0)
    refs[-1][...] = before[...] + pull(factors, fixed[...], block)


def on_diagonal(rows):
    shape = (rows, rows)
    return lax.broadcasted_iota(jnp.int32, shape, 0) == lax.broadcasted_iota(jnp.int32, shape, 1)


def last_sum(factors, fixed, before, far_opposite, inv, keep, inner_kept, give):
    core, chip = position()
    rows, width = fixed.shape
    span = width // 4
    cut = span // LANES * LANES
    chip0 = chip == 0
    a = fixed[...]
    total = before[...] + pull(factors, a, far_opposite[...])
    unit = a.astype(F32)
    by_row = factors[0:1, 0:1] * inv[...]
    inner = jnp.sum(unit * total, axis=1, keepdims=True) * by_row
    across = total * by_row - unit * inner
    middle = 4 * cut + 2 * (span - cut)
    first = jnp.concatenate([across[:, : 2 * cut], across[:, 4 * cut : middle]], axis=1)
    last = jnp.concatenate([across[:, 2 * cut : 4 * cut], across[:, middle:]], axis=1)
    keep[...] = jnp.where(chip0, first, last)
    inner_kept[...] = inner
    pack(give, 0, jnp.where(chip0, last, first).astype(BF16))
    at = packed_rows(rows, 2 * span)
    line = jnp.sum(jnp.where(on_diagonal(rows), inner, 0.0), axis=0, keepdims=True)
    give[at : at + 16, :] = jnp.broadcast_to(line[:, :LANES], (16, LANES)).astype(BF16)
    give[at + 16 : at + 32, :] = jnp.broadcast_to(line[:, rows - LANES :], (16, LANES)).astype(BF16)


def finish_sum(kept, inner_kept, got, rest_mine, rest_peer, stacked):
    rows, width = kept.shape
    at = packed_rows(rows, width)
    start, end = got[at : at + 1, :], got[at + 16 : at + 17, :]
    line = jnp.concatenate([start, end[:, 2 * LANES - rows :]], axis=1).astype(F32)
    other = jnp.sum(jnp.where(on_diagonal(rows), line, 0.0), axis=1, keepdims=True)
    rest = beside([rest_mine[...], rest_peer[...]], 1).astype(F32)
    demb = kept[...] + unpack(got, 0, rows, width).astype(F32) - rest * (inner_kept[...] + other)
    high = demb.astype(BF16)
    stacked[:rows, :] = high
    stacked[rows:, :] = (demb - high.astype(F32)).astype(BF16)


def through_matrix(
    kept, inner_kept, got, rest_mine, rest_peer, mine, peer, to_chip, to_cross, to_core, keep, stacked
):
    core, chip = position()
    rows, width = kept.shape
    span = width // 2
    finish_sum(kept, inner_kept, got, rest_mine, rest_peer, stacked)
    matrix = beside([mine[...], peer[...]], 0)
    part = jnp.dot(stacked[...], matrix, preferred_element_type=F32)
    part = part[:rows] + part[rows:]
    spans = [part[:, u * span : (u + 1) * span] for u in range(4)]
    for t in range(4):

        @pl.when(2 * chip + core == t)
        def _(t=t):
            pack(to_chip, 0, spans[t ^ 2].astype(BF16))
            pack(to_cross, 0, spans[t ^ 3].astype(BF16))
            pack(to_core, 0, spans[t ^ 1].astype(BF16))
            keep[...] = spans[t]


def last_add(from_chip, from_cross, from_core, kept, img, txt):
    core, chip = position()
    rows, span = kept.shape
    core0 = core == 0
    mine = kept[...] + unpack(from_chip, 0, rows, span).astype(F32)
    theirs = unpack(from_core, 0, rows, span).astype(F32)
    theirs = theirs + unpack(from_cross, 0, rows, span).astype(F32)
    img[...] = jnp.where(core0, mine, theirs)
    txt[...] = jnp.where(core0, theirs, mine)


def shards(
    picture_averaged_vectors,
    picture_mapping_matrix,
    caption_averaged_vectors,
    caption_mapping_matrix,
    sharpness_factor,
    offset_term,
    paired_caption_index,
):
    groups = lax.axis_size("dp")
    rows = picture_averaged_vectors.shape[0]
    half = rows // 2
    span = picture_mapping_matrix.shape[1]
    width = 4 * span
    t = lax.axis_index("tensor")
    core0 = t % 2 == 0
    chip0 = t < 2
    factors = jnp.concatenate([sharpness_factor, offset_term])
    factors = jnp.broadcast_to(factors[:, None], (2, LANES))

    img_emb = jnp.dot(
        picture_averaged_vectors, picture_mapping_matrix, preferred_element_type=F32
    )
    txt_emb = jnp.dot(
        caption_averaged_vectors, caption_mapping_matrix, preferred_element_type=F32
    )
    squares = jnp.concatenate(
        [jnp.sum(img_emb * img_emb, axis=1), jnp.sum(txt_emb * txt_emb, axis=1)]
    )
    inv = lax.rsqrt(lax.psum(squares, "tensor") + 1e-06)
    inv_img, inv_txt = inv[:rows], inv[rows:]
    img_unit = img_emb * inv_img[:, None]
    txt_unit = txt_emb * inv_txt[:, None]
    piece = ((rows, span), BF16)
    own, fixed_own, moving_own, rest_mine, rest_theirs = call(
        unit_parts,
        [((2 * packed_rows(rows, span), LANES), BF16)] + [piece] * 4,
        img_unit,
        txt_unit,
    )
    other = exchange(own, groups, chip_swap)
    rest_peer = exchange(rest_theirs, groups, core_swap)
    img_matrix, txt_matrix, _ = lax.optimization_barrier(
        (picture_mapping_matrix.T, caption_mapping_matrix.T, own)
    )
    matrix_mine = jnp.where(core0, img_matrix, txt_matrix)
    matrix_theirs = jnp.where(core0, txt_matrix, img_matrix)
    matrix_peer = exchange(matrix_theirs, groups, core_swap)
    (pair,) = call(pair_up, [((2 * rows, 2 * span), BF16)], fixed_own, moving_own, other)
    peer = exchange(pair, groups, core_swap)
    peer, matrix_peer = lax.optimization_barrier((peer, matrix_peer))
    half_width = ((half, width), BF16)
    (other_half,) = call(relayed_half, [half_width], pair, peer)
    pair, peer, other_half = lax.optimization_barrier((pair, peer, other_half))
    fixed, own_half = call(fixed_and_half, [((rows, width), BF16), half_width], pair, peer)
    inv_fixed = jnp.where(core0, inv_img, inv_txt)[:, None]

    first_row = lax.axis_index("dp") * rows
    ids = first_row + jnp.arange(rows, dtype=jnp.int32)
    half_ids = jnp.where(chip0, ids[:half], ids[half:])
    half_index = jnp.where(chip0, paired_caption_index[:half], paired_caption_index[half:])
    matched = jnp.where(
        core0,
        paired_caption_index[:, None] == half_ids[None, :],
        ids[:, None] == half_index[None, :],
    )
    sign = jnp.where(matched, 1.0, -1.0).astype(F32)

    sums = [((rows, width), F32)]
    near_relayed = exchange(other_half, groups, neighbour)
    near_other = exchange(own_half, groups, neighbour)
    (total,) = call(first_sum, sums, factors, fixed, sign, own_half)
    near_relayed, total = lax.optimization_barrier((near_relayed, total))
    opposite = exchange(near_relayed, groups, relay)
    far_own = exchange(own_half, groups, beyond)
    far_relayed = exchange(near_relayed, groups, beyond)
    far_other = exchange(near_other, groups, beyond)
    far_opposite = exchange(opposite, groups, beyond)
    nearer = (near_relayed, near_other, opposite)
    (total,) = call(
        next_sum, sums, factors, fixed, total, *nearer, far_own, far_relayed, far_other
    )
    keep, inner_kept, give = call(
        last_sum,
        [
            ((rows, 2 * span), F32),
            ((rows, 1), F32),
            ((packed_rows(rows, 2 * span) + 32, LANES), BF16),
        ],
        factors,
        fixed,
        total,
        far_opposite,
        inv_fixed,
    )
    got = exchange(give, groups, chip_swap)
    part = ((rows, span), F32)
    sent = ((packed_rows(rows, span), LANES), BF16)
    to_chip, to_cross, to_core, keep = call(
        through_matrix,
        [sent, sent, sent, part],
        keep,
        inner_kept,
        got,
        rest_mine,
        rest_peer,
        matrix_mine,
        matrix_peer,
        scratch=[((2 * rows, 2 * span), BF16)],
    )
    from_chip = exchange(to_chip, groups, chip_swap)
    from_cross = exchange(to_cross, groups, cross_swap)
    from_core = exchange(to_core, groups, core_swap)
    return tuple(call(last_add, [part, part], from_chip, from_cross, from_core, keep))


def solution(mesh):
    in_specs = (
        P("dp", None),
        P(None, "tensor"),
        P("dp", None),
        P(None, "tensor"),
        P(),
        P(),
        P("dp"),
    )
    out_specs = (P("dp", "tensor"), P("dp", "tensor"))
    return jax.shard_map(shards, mesh=mesh, in_specs=in_specs, out_specs=out_specs, check_vma=False)
```

```python
import jax
import jax.numpy as jnp
from jax import lax
from jax.experimental import pallas as pl
from jax.experimental.pallas import tpu as pltpu
from jax.sharding import PartitionSpec as P

AXES = ("dp", "tensor")
ROUND = 4
LANES = 128
F32, F16, BF16 = jnp.float32, jnp.float16, jnp.bfloat16
RAISED = 32.0
BY_COLUMNS = (((1,), (1,)), ((), ()))


def exchange(block, groups, source):
    route = []
    for n in range(groups):
        for t in range(4):
            m, u = source(n, t)
            route.append(((m % groups) * 4 + u, n * 4 + t))
    return lax.ppermute(block, AXES, route)


def neighbour(n, t):
    return [(n + 3, 2), (n - 1, 3), (n + 1, 0), (n - 3, 1)][t]


def relay(n, t):
    return (n - 1, t) if t < 2 else (n + 1, t)


def beyond(n, t):
    return (n + ROUND, t) if t % 2 == 0 else (n - ROUND, t)


def chip_swap(n, t):
    return (n, t ^ 2)


def core_swap(n, t):
    return (n, t ^ 1)


def cross_swap(n, t):
    return (n, t ^ 3)


def position():
    t = lax.axis_index("tensor")
    return lax.rem(t, 2), lax.div(t, 2)


def call(kernel, outs, *operands, scratch=(), flops=0):
    specs = [
        pl.BlockSpec(memory_space=pltpu.SMEM if x.ndim == 1 else pltpu.VMEM) for x in operands
    ]
    moved = sum(x.size * x.dtype.itemsize for x in operands)
    return pl.pallas_call(
        kernel,
        cost_estimate=pl.CostEstimate(flops=flops, bytes_accessed=moved, transcendentals=0),
        out_shape=[jax.ShapeDtypeStruct(shape, dtype) for shape, dtype in outs],
        in_specs=specs,
        out_specs=[pl.BlockSpec(memory_space=pltpu.VMEM)] * len(outs),
        scratch_shapes=[pltpu.VMEM(shape, dtype) for shape, dtype in scratch],
        compiler_params=pltpu.CompilerParams(vmem_limit_bytes=24 * 2**20),
    )(*operands)


def packed_rows(rows, columns):
    whole, rest = columns // LANES, columns % LANES
    return rows * whole + (rows * rest) // LANES


def pack(ref, at, value):
    rows, columns = value.shape
    whole, rest = columns // LANES, columns % LANES
    for i in range(whole):
        ref[at + i * rows : at + (i + 1) * rows, :] = value[:, i * LANES : (i + 1) * LANES]
    if rest:
        side = LANES // rest
        short = rows // side
        at = at + whole * rows
        ref[at : at + short, :] = jnp.concatenate(
            [value[i * short : (i + 1) * short, whole * LANES :] for i in range(side)], axis=1
        )


def unpack(ref, at, rows, columns):
    whole, rest = columns // LANES, columns % LANES
    tiles = [ref[at + i * rows : at + (i + 1) * rows, :] for i in range(whole)]
    if rest:
        side = LANES // rest
        short = rows // side
        last = ref[at + whole * rows : at + whole * rows + short, :]
        tiles.append(
            jnp.concatenate([last[:, i * rest : (i + 1) * rest] for i in range(side)], axis=0)
        )
    return jnp.concatenate(tiles, axis=1)


def beside(parts, axis):
    cut = parts[0].shape[axis] // LANES * LANES
    size = parts[0].shape[axis]
    return jnp.concatenate(
        [lax.slice_in_dim(x, 0, cut, axis=axis) for x in parts]
        + [lax.slice_in_dim(x, cut, size, axis=axis) for x in parts],
        axis=axis,
    )


def embedded(img, txt, own, fixed, moving):
    core, _ = position()
    rows, span = img.shape
    a, b = img[...], txt[...]
    keep = jnp.where(core == 0, a, b) * RAISED
    travel = jnp.where(core == 0, b, a) * RAISED
    fixed[...] = keep
    moving[...] = travel
    pack(own, 0, keep)
    pack(own, packed_rows(rows, span), travel)


def pair_up(fixed, moving, got, pair):
    _, chip = position()
    rows, span = fixed.shape
    second = packed_rows(rows, span)
    for i, ref in enumerate((fixed, moving)):
        own, other = ref[...], unpack(got, i * second, rows, span)
        first, last = jnp.where(chip == 0, own, other), jnp.where(chip == 0, other, own)
        fill = jnp.zeros((rows, pair.shape[1] - 2 * span), F32)
        pair[i * rows : (i + 1) * rows, :] = jnp.concatenate(
            [beside([first, last], 1), fill], axis=1
        )


def widened(mine, theirs, span):
    cut = span // LANES * LANES
    middle, end = cut + span, 2 * span
    return jnp.concatenate(
        [mine[:, :cut], theirs[:, :cut], mine[:, cut : 2 * cut], theirs[:, cut : 2 * cut]]
        + [mine[:, 2 * cut : middle], theirs[:, 2 * cut : middle]]
        + [mine[:, middle:end], theirs[:, middle:end]],
        axis=1,
    )


def unit_rows(emb):
    inv = lax.rsqrt(jnp.sum(emb * emb, axis=1, keepdims=True) + 1e-06 * RAISED**2)
    return emb * inv, inv * RAISED


def wide_half(own, pair, peer, out):
    half = out.shape[0]
    rows = 2 * half
    _, chip = position()
    for first in (True, False):

        @pl.when((chip == 0) == (first == own))
        def _(first=first):
            at = 0 if first else half
            mine, theirs = pair[rows + at : rows + at + half, :], peer[at : at + half, :]
            unit, _ = unit_rows(widened(mine, theirs, out.shape[1] // 4))
            out[...] = unit.astype(BF16)


def relayed_half(pair, peer, other_half):
    wide_half(False, pair, peer, other_half)


def fixed_and_half(pair, peer, fixed, own_half, unit, inv):
    rows, width = fixed.shape
    wide = widened(pair[:rows, :], peer[rows:, :], width // 4)
    unit[...], inv[...] = unit_rows(wide)
    fixed[...] = unit[...].astype(BF16)
    wide_half(True, pair, peer, own_half)


def pull(factors, fixed, block, sign=None):
    logits = factors[0:1, 0:1] * lax.dot_general(
        fixed, block, BY_COLUMNS, preferred_element_type=F32
    ) + factors[1:2, 0:1]
    if sign is None:
        weight = 16.0 * jax.nn.sigmoid(logits)
    else:
        weight = -16.0 * sign * jax.nn.sigmoid(-sign * logits)
    return jnp.dot(weight.astype(BF16), block, preferred_element_type=F32)


def first_sum(factors, fixed, sign, own_half, total):
    total[...] = pull(factors, fixed[...], own_half[...], sign[...])


def next_sum(factors, fixed, before, *refs):
    block = jnp.concatenate([x[...] for x in refs[:-1]], axis=0)
    refs[-1][...] = before[...] + pull(factors, fixed[...], block)


def last_sum(factors, fixed, before, far_opposite, unit, inv, keep, give):
    _, chip = position()
    rows, width = fixed.shape
    span = width // 4
    cut = span // LANES * LANES
    total = before[...] + pull(factors, fixed[...], far_opposite[...])
    inner = jnp.sum(unit[...] * total, axis=1, keepdims=True)
    across = (total - unit[...] * inner) * (factors[0:1, 0:1] * inv[...])
    middle = 4 * cut + 2 * (span - cut)
    first = jnp.concatenate([across[:, : 2 * cut], across[:, 4 * cut : middle]], axis=1)
    last = jnp.concatenate([across[:, 2 * cut : 4 * cut], across[:, middle:]], axis=1)
    keep[...] = jnp.where(chip == 0, first, last)
    pack(give, 0, jnp.where(chip == 0, last, first).astype(BF16))


def through_matrix(kept, got, mine, peer, to_chip, to_cross, to_core, keep, stacked):
    core, chip = position()
    rows, width = kept.shape
    span = width // 2
    demb = kept[...] + unpack(got, 0, rows, width).astype(F32)
    high = demb.astype(BF16)
    stacked[:rows, :] = high
    stacked[rows:, :] = (demb - high.astype(F32)).astype(BF16)
    matrix = beside([mine[...], peer[...]], 0)
    part = jnp.dot(stacked[...], matrix, preferred_element_type=F32)
    part = part[:rows] + part[rows:]
    spans = [part[:, u * span : (u + 1) * span] for u in range(4)]
    for t in range(4):

        @pl.when(2 * chip + core == t)
        def _(t=t):
            pack(to_chip, 0, spans[t ^ 2].astype(BF16))
            pack(to_cross, 0, spans[t ^ 3].astype(BF16))
            pack(to_core, 0, spans[t ^ 1].astype(BF16))
            keep[...] = spans[t]


def last_add(from_chip, from_cross, from_core, kept, img, txt):
    core, chip = position()
    rows, span = kept.shape
    core0 = core == 0
    mine = kept[...] + unpack(from_chip, 0, rows, span).astype(F32)
    theirs = unpack(from_core, 0, rows, span).astype(F32)
    theirs = theirs + unpack(from_cross, 0, rows, span).astype(F32)
    img[...] = jnp.where(core0, mine, theirs)
    txt[...] = jnp.where(core0, theirs, mine)


def shards(
    picture_averaged_vectors,
    picture_mapping_matrix,
    caption_averaged_vectors,
    caption_mapping_matrix,
    sharpness_factor,
    offset_term,
    paired_caption_index,
):
    groups = lax.axis_size("dp")
    rows = picture_averaged_vectors.shape[0]
    half = rows // 2
    span = picture_mapping_matrix.shape[1]
    width = 4 * span
    t = lax.axis_index("tensor")
    core0 = t % 2 == 0
    chip0 = t < 2
    factors = jnp.concatenate([sharpness_factor, offset_term])
    factors = jnp.broadcast_to(factors[:, None], (2, LANES))

    img_emb = jnp.dot(
        picture_averaged_vectors, picture_mapping_matrix, preferred_element_type=F32
    )
    txt_emb = jnp.dot(
        caption_averaged_vectors, caption_mapping_matrix, preferred_element_type=F32
    )
    emb_piece = ((rows, span), F32)
    own, fixed_own, moving_own = call(
        embedded,
        [((2 * packed_rows(rows, span), LANES), F32), emb_piece, emb_piece],
        img_emb,
        txt_emb,
    )
    sent = own.astype(F16)
    other = exchange(sent, groups, chip_swap).astype(F32)
    img_matrix, txt_matrix, _ = lax.optimization_barrier(
        (picture_mapping_matrix.T, caption_mapping_matrix.T, sent)
    )
    matrix_mine = jnp.where(core0, img_matrix, txt_matrix)
    matrix_theirs = jnp.where(core0, txt_matrix, img_matrix)
    matrix_peer = exchange(matrix_theirs, groups, core_swap)
    pair_width = 2 * (span // LANES * LANES) + LANES
    (pair,) = call(pair_up, [((2 * rows, pair_width), F32)], fixed_own, moving_own, other)
    peer = exchange(pair.astype(F16), groups, core_swap)
    peer, matrix_peer = lax.optimization_barrier((peer, matrix_peer))
    peer = peer.astype(F32)
    half_width = ((half, width), BF16)
    (other_half,) = call(relayed_half, [half_width], pair, peer)
    pair, peer, other_half = lax.optimization_barrier((pair, peer, other_half))
    fixed, own_half, unit, inv = call(
        fixed_and_half,
        [((rows, width), BF16), half_width, ((rows, width), F32), ((rows, 1), F32)],
        pair,
        peer,
    )

    first_row = lax.axis_index("dp") * rows
    ids = first_row + jnp.arange(rows, dtype=jnp.int32)
    half_ids = jnp.where(chip0, ids[:half], ids[half:])
    half_index = jnp.where(chip0, paired_caption_index[:half], paired_caption_index[half:])
    matched = jnp.where(
        core0,
        paired_caption_index[:, None] == half_ids[None, :],
        ids[:, None] == half_index[None, :],
    )
    sign = jnp.where(matched, 1.0, -1.0).astype(F32)

    sums = [((rows, width), F32)]
    near_relayed = exchange(other_half, groups, neighbour)
    near_other = exchange(own_half, groups, neighbour)
    (total,) = call(first_sum, sums, factors, fixed, sign, own_half)
    near_relayed, total = lax.optimization_barrier((near_relayed, total))
    opposite = exchange(near_relayed, groups, relay)
    far_own = exchange(own_half, groups, beyond)
    far_relayed = exchange(near_relayed, groups, beyond)
    far_other = exchange(near_other, groups, beyond)
    far_opposite = exchange(opposite, groups, beyond)
    nearer = (near_relayed, near_other, opposite)
    (total,) = call(
        next_sum, sums, factors, fixed, total, *nearer, far_own, far_relayed, far_other
    )
    keep, give = call(
        last_sum,
        [((rows, 2 * span), F32), ((packed_rows(rows, 2 * span), LANES), BF16)],
        factors,
        fixed,
        total,
        far_opposite,
        unit,
        inv,
    )
    got = exchange(give, groups, chip_swap)
    part = ((rows, span), F32)
    sent = ((packed_rows(rows, span), LANES), BF16)
    to_chip, to_cross, to_core, keep = call(
        through_matrix,
        [sent, sent, sent, part],
        keep,
        got,
        matrix_mine,
        matrix_peer,
        scratch=[((2 * rows, 2 * span), BF16)],
    )
    from_chip = exchange(to_chip, groups, chip_swap)
    from_cross = exchange(to_cross, groups, cross_swap)
    from_core = exchange(to_core, groups, core_swap)
    return tuple(call(last_add, [part, part], from_chip, from_cross, from_core, keep))


def solution(mesh):
    in_specs = (
        P("dp", None),
        P(None, "tensor"),
        P("dp", None),
        P(None, "tensor"),
        P(),
        P(),
        P("dp"),
    )
    out_specs = (P("dp", "tensor"), P("dp", "tensor"))
    return jax.shard_map(shards, mesh=mesh, in_specs=in_specs, out_specs=out_specs, check_vma=False)
```

```python
import jax
import jax.numpy as jnp
from jax import lax
from jax.experimental import pallas as pl
from jax.experimental.pallas import tpu as pltpu
from jax.sharding import PartitionSpec as P

AXES = ("dp", "tensor")
ROUND = 4
LANES = 128
F32, F16, BF16 = jnp.float32, jnp.float16, jnp.bfloat16
RAISED = 32.0
BY_COLUMNS = (((1,), (1,)), ((), ()))


def exchange(block, groups, source):
    route = []
    for n in range(groups):
        for t in range(4):
            m, u = source(n, t)
            route.append(((m % groups) * 4 + u, n * 4 + t))
    return lax.ppermute(block, AXES, route)


def neighbour(n, t):
    return [(n + 3, 2), (n - 1, 3), (n + 1, 0), (n - 3, 1)][t]


def relay(n, t):
    return (n - 1, t) if t < 2 else (n + 1, t)


def beyond(n, t):
    return (n + ROUND, t) if t % 2 == 0 else (n - ROUND, t)


def chip_swap(n, t):
    return (n, t ^ 2)


def core_swap(n, t):
    return (n, t ^ 1)


def cross_swap(n, t):
    return (n, t ^ 3)


def position():
    t = lax.axis_index("tensor")
    return lax.rem(t, 2), lax.div(t, 2)


def call(kernel, outs, *operands, scratch=(), flops=0):
    specs = [
        pl.BlockSpec(memory_space=pltpu.SMEM if x.ndim == 1 else pltpu.VMEM) for x in operands
    ]
    moved = sum(x.size * x.dtype.itemsize for x in operands)
    return pl.pallas_call(
        kernel,
        cost_estimate=pl.CostEstimate(flops=flops, bytes_accessed=moved, transcendentals=0),
        out_shape=[jax.ShapeDtypeStruct(shape, dtype) for shape, dtype in outs],
        in_specs=specs,
        out_specs=[pl.BlockSpec(memory_space=pltpu.VMEM)] * len(outs),
        scratch_shapes=[pltpu.VMEM(shape, dtype) for shape, dtype in scratch],
        compiler_params=pltpu.CompilerParams(vmem_limit_bytes=24 * 2**20),
    )(*operands)


def packed_rows(rows, columns):
    whole, rest = columns // LANES, columns % LANES
    return rows * whole + (rows * rest) // LANES


def pack(ref, at, value):
    rows, columns = value.shape
    whole, rest = columns // LANES, columns % LANES
    for i in range(whole):
        ref[at + i * rows : at + (i + 1) * rows, :] = value[:, i * LANES : (i + 1) * LANES]
    if rest:
        side = LANES // rest
        short = rows // side
        at = at + whole * rows
        ref[at : at + short, :] = jnp.concatenate(
            [value[i * short : (i + 1) * short, whole * LANES :] for i in range(side)], axis=1
        )


def unpack(ref, at, rows, columns):
    whole, rest = columns // LANES, columns % LANES
    tiles = [ref[at + i * rows : at + (i + 1) * rows, :] for i in range(whole)]
    if rest:
        side = LANES // rest
        short = rows // side
        last = ref[at + whole * rows : at + whole * rows + short, :]
        tiles.append(
            jnp.concatenate([last[:, i * rest : (i + 1) * rest] for i in range(side)], axis=0)
        )
    return jnp.concatenate(tiles, axis=1)


def beside(parts, axis):
    cut = parts[0].shape[axis] // LANES * LANES
    size = parts[0].shape[axis]
    return jnp.concatenate(
        [lax.slice_in_dim(x, 0, cut, axis=axis) for x in parts]
        + [lax.slice_in_dim(x, cut, size, axis=axis) for x in parts],
        axis=axis,
    )


def embedded(img, txt, own, fixed, moving):
    core, _ = position()
    rows, span = img.shape
    a, b = img[...], txt[...]
    keep = jnp.where(core == 0, a, b) * RAISED
    travel = jnp.where(core == 0, b, a) * RAISED
    fixed[...] = keep
    moving[...] = travel
    pack(own, 0, keep)
    pack(own, packed_rows(rows, span), travel)


def pair_up(fixed, moving, got, pair):
    _, chip = position()
    rows, span = fixed.shape
    second = packed_rows(rows, span)
    for i, ref in enumerate((fixed, moving)):
        own, other = ref[...], unpack(got, i * second, rows, span)
        first, last = jnp.where(chip == 0, own, other), jnp.where(chip == 0, other, own)
        fill = jnp.zeros((rows, pair.shape[1] - 2 * span), F32)
        pair[i * rows : (i + 1) * rows, :] = jnp.concatenate(
            [beside([first, last], 1), fill], axis=1
        )


def widened(mine, theirs, span):
    cut = span // LANES * LANES
    middle, end = cut + span, 2 * span
    return jnp.concatenate(
        [mine[:, :cut], theirs[:, :cut], mine[:, cut : 2 * cut], theirs[:, cut : 2 * cut]]
        + [mine[:, 2 * cut : middle], theirs[:, 2 * cut : middle]]
        + [mine[:, middle:end], theirs[:, middle:end]],
        axis=1,
    )


def unit_rows(emb):
    inv = lax.rsqrt(jnp.sum(emb * emb, axis=1, keepdims=True) + 1e-06 * RAISED**2)
    return emb * inv, inv * RAISED


def wide_half(own, pair, peer, out):
    half = out.shape[0]
    rows = 2 * half
    _, chip = position()
    for first in (True, False):

        @pl.when((chip == 0) == (first == own))
        def _(first=first):
            at = 0 if first else half
            mine, theirs = pair[rows + at : rows + at + half, :], peer[at : at + half, :]
            unit, _ = unit_rows(widened(mine, theirs, out.shape[1] // 4))
            out[...] = unit.astype(BF16)


def relayed_half(pair, peer, other_half):
    wide_half(False, pair, peer, other_half)


def fixed_and_half(pair, peer, fixed, own_half, unit, inv):
    rows, width = fixed.shape
    wide = widened(pair[:rows, :], peer[rows:, :], width // 4)
    unit[...], inv[...] = unit_rows(wide)
    fixed[...] = unit[...].astype(BF16)
    wide_half(True, pair, peer, own_half)


def pull(factors, fixed, block, sign=None):
    logits = factors[0:1, 0:1] * lax.dot_general(
        fixed, block, BY_COLUMNS, preferred_element_type=F32
    ) + factors[1:2, 0:1]
    if sign is None:
        weight = 16.0 * jax.nn.sigmoid(logits)
    else:
        weight = -16.0 * sign * jax.nn.sigmoid(-sign * logits)
    return jnp.dot(weight.astype(BF16), block, preferred_element_type=F32)


def first_sum(factors, fixed, sign, own_half, total):
    total[...] = pull(factors, fixed[...], own_half[...], sign[...])


def next_sum(factors, fixed, before, *refs):
    block = jnp.concatenate([x[...] for x in refs[:-1]], axis=0)
    refs[-1][...] = before[...] + pull(factors, fixed[...], block)


def last_sum(factors, fixed, before, far_opposite, unit, inv, keep, give):
    _, chip = position()
    rows, width = fixed.shape
    span = width // 4
    cut = span // LANES * LANES
    total = before[...] + pull(factors, fixed[...], far_opposite[...])
    inner = jnp.sum(unit[...] * total, axis=1, keepdims=True)
    across = (total - unit[...] * inner) * (factors[0:1, 0:1] * inv[...])
    middle = 4 * cut + 2 * (span - cut)
    first = jnp.concatenate([across[:, : 2 * cut], across[:, 4 * cut : middle]], axis=1)
    last = jnp.concatenate([across[:, 2 * cut : 4 * cut], across[:, middle:]], axis=1)
    keep[...] = jnp.where(chip == 0, first, last)
    pack(give, 0, jnp.where(chip == 0, last, first).astype(BF16))


def through_matrix(kept, got, mine, peer, to_chip, to_cross, to_core, keep, stacked):
    core, chip = position()
    rows, width = kept.shape
    span = width // 2
    demb = kept[...] + unpack(got, 0, rows, width).astype(F32)
    high = demb.astype(BF16)
    stacked[:rows, :] = high
    stacked[rows:, :] = (demb - high.astype(F32)).astype(BF16)
    matrix = beside([mine[...], peer[...]], 0)
    part = jnp.dot(stacked[...], matrix, preferred_element_type=F32)
    part = part[:rows] + part[rows:]
    spans = [part[:, u * span : (u + 1) * span] for u in range(4)]
    for t in range(4):

        @pl.when(2 * chip + core == t)
        def _(t=t):
            pack(to_chip, 0, spans[t ^ 2].astype(BF16))
            pack(to_cross, 0, spans[t ^ 3].astype(BF16))
            pack(to_core, 0, spans[t ^ 1].astype(BF16))
            keep[...] = spans[t]


def last_add(from_chip, from_cross, from_core, kept, img, txt):
    core, chip = position()
    rows, span = kept.shape
    core0 = core == 0
    mine = kept[...] + unpack(from_chip, 0, rows, span).astype(F32)
    theirs = unpack(from_core, 0, rows, span).astype(F32)
    theirs = theirs + unpack(from_cross, 0, rows, span).astype(F32)
    img[...] = jnp.where(core0, mine, theirs)
    txt[...] = jnp.where(core0, theirs, mine)


def shards(
    picture_averaged_vectors,
    picture_mapping_matrix,
    caption_averaged_vectors,
    caption_mapping_matrix,
    sharpness_factor,
    offset_term,
    paired_caption_index,
):
    groups = lax.axis_size("dp")
    rows = picture_averaged_vectors.shape[0]
    half = rows // 2
    span = picture_mapping_matrix.shape[1]
    width = 4 * span
    t = lax.axis_index("tensor")
    core0 = t % 2 == 0
    chip0 = t < 2
    factors = jnp.concatenate([sharpness_factor, offset_term])
    factors = jnp.broadcast_to(factors[:, None], (2, LANES))

    img_emb = jnp.dot(
        picture_averaged_vectors, picture_mapping_matrix, preferred_element_type=F32
    )
    txt_emb = jnp.dot(
        caption_averaged_vectors, caption_mapping_matrix, preferred_element_type=F32
    )
    emb_piece = ((rows, span), F32)
    own, fixed_own, moving_own = call(
        embedded,
        [((2 * packed_rows(rows, span), LANES), F32), emb_piece, emb_piece],
        img_emb,
        txt_emb,
    )
    sent = own.astype(F16)
    other = exchange(sent, groups, chip_swap).astype(F32)
    img_matrix, txt_matrix, _ = lax.optimization_barrier(
        (picture_mapping_matrix.T, caption_mapping_matrix.T, sent)
    )
    matrix_mine = jnp.where(core0, img_matrix, txt_matrix)
    matrix_theirs = jnp.where(core0, txt_matrix, img_matrix)
    matrix_peer = exchange(matrix_theirs, groups, core_swap)
    first_row = lax.axis_index("dp") * rows
    ids = first_row + jnp.arange(rows, dtype=jnp.int32)
    half_ids = jnp.where(chip0, ids[:half], ids[half:])
    half_index = jnp.where(chip0, paired_caption_index[:half], paired_caption_index[half:])
    matched = jnp.where(
        core0,
        paired_caption_index[:, None] == half_ids[None, :],
        ids[:, None] == half_index[None, :],
    )
    sign = jnp.where(matched, 1.0, -1.0).astype(F32)
    other, sign = lax.optimization_barrier((other, sign))
    pair_width = 2 * (span // LANES * LANES) + LANES
    (pair,) = call(pair_up, [((2 * rows, pair_width), F32)], fixed_own, moving_own, other)
    peer = exchange(pair.astype(F16), groups, core_swap)
    peer, matrix_peer = lax.optimization_barrier((peer, matrix_peer))
    peer = peer.astype(F32)
    half_width = ((half, width), BF16)
    (other_half,) = call(relayed_half, [half_width], pair, peer)
    pair, peer, other_half = lax.optimization_barrier((pair, peer, other_half))
    fixed, own_half, unit, inv = call(
        fixed_and_half,
        [((rows, width), BF16), half_width, ((rows, width), F32), ((rows, 1), F32)],
        pair,
        peer,
    )

    sums = [((rows, width), F32)]
    near_relayed = exchange(other_half, groups, neighbour)
    far_own = exchange(own_half, groups, beyond)
    near_other = exchange(own_half, groups, neighbour)
    (total,) = call(first_sum, sums, factors, fixed, sign, own_half)
    near_relayed, total = lax.optimization_barrier((near_relayed, total))
    opposite = exchange(near_relayed, groups, relay)
    far_own, near_sent = lax.optimization_barrier((far_own, near_relayed))
    far_relayed = exchange(near_sent, groups, beyond)
    far_other = exchange(near_other, groups, beyond)
    (total,) = call(next_sum, sums, factors, fixed, total, far_own, near_relayed, near_other)
    opposite, total = lax.optimization_barrier((opposite, total))
    far_opposite = exchange(opposite, groups, beyond)
    (total,) = call(next_sum, sums, factors, fixed, total, opposite, far_relayed, far_other)
    keep, give = call(
        last_sum,
        [((rows, 2 * span), F32), ((packed_rows(rows, 2 * span), LANES), BF16)],
        factors,
        fixed,
        total,
        far_opposite,
        unit,
        inv,
    )
    got = exchange(give, groups, chip_swap)
    part = ((rows, span), F32)
    sent = ((packed_rows(rows, span), LANES), BF16)
    to_chip, to_cross, to_core, keep = call(
        through_matrix,
        [sent, sent, sent, part],
        keep,
        got,
        matrix_mine,
        matrix_peer,
        scratch=[((2 * rows, 2 * span), BF16)],
    )
    from_chip = exchange(to_chip, groups, chip_swap)
    from_cross = exchange(to_cross, groups, cross_swap)
    from_core = exchange(to_core, groups, core_swap)
    return tuple(call(last_add, [part, part], from_chip, from_cross, from_core, keep))


def solution(mesh):
    in_specs = (
        P("dp", None),
        P(None, "tensor"),
        P("dp", None),
        P(None, "tensor"),
        P(),
        P(),
        P("dp"),
    )
    out_specs = (P("dp", "tensor"), P("dp", "tensor"))
    return jax.shard_map(shards, mesh=mesh, in_specs=in_specs, out_specs=out_specs, check_vma=False)
```

```python
import jax
import jax.numpy as jnp
from jax import lax
from jax.experimental import pallas as pl
from jax.experimental.pallas import tpu as pltpu
from jax.sharding import PartitionSpec as P

AXES = ("dp", "tensor")
ROUND = 4
LANES = 128
F32, F16, BF16 = jnp.float32, jnp.float16, jnp.bfloat16
RAISED = 32.0
BY_COLUMNS = (((1,), (1,)), ((), ()))


def exchange(block, groups, source):
    route = []
    for n in range(groups):
        for t in range(4):
            m, u = source(n, t)
            route.append(((m % groups) * 4 + u, n * 4 + t))
    return lax.ppermute(block, AXES, route)


def neighbour(n, t):
    return [(n + 3, 2), (n - 1, 3), (n + 1, 0), (n - 3, 1)][t]


def relay(n, t):
    return (n - 1, t) if t < 2 else (n + 1, t)


def beyond(n, t):
    return (n + ROUND, t) if t % 2 == 0 else (n - ROUND, t)


def chip_swap(n, t):
    return (n, t ^ 2)


def core_swap(n, t):
    return (n, t ^ 1)


def cross_swap(n, t):
    return (n, t ^ 3)


def position():
    t = lax.axis_index("tensor")
    return lax.rem(t, 2), lax.div(t, 2)


def call(kernel, outs, *operands, scratch=(), flops=0):
    specs = [
        pl.BlockSpec(memory_space=pltpu.SMEM if x.ndim == 1 else pltpu.VMEM) for x in operands
    ]
    moved = sum(x.size * x.dtype.itemsize for x in operands)
    return pl.pallas_call(
        kernel,
        cost_estimate=pl.CostEstimate(flops=flops, bytes_accessed=moved, transcendentals=0),
        out_shape=[jax.ShapeDtypeStruct(shape, dtype) for shape, dtype in outs],
        in_specs=specs,
        out_specs=[pl.BlockSpec(memory_space=pltpu.VMEM)] * len(outs),
        scratch_shapes=[pltpu.VMEM(shape, dtype) for shape, dtype in scratch],
        compiler_params=pltpu.CompilerParams(vmem_limit_bytes=24 * 2**20),
    )(*operands)


def packed_rows(rows, columns):
    whole, rest = columns // LANES, columns % LANES
    return rows * whole + (rows * rest) // LANES


def pack(ref, at, value):
    rows, columns = value.shape
    whole, rest = columns // LANES, columns % LANES
    for i in range(whole):
        ref[at + i * rows : at + (i + 1) * rows, :] = value[:, i * LANES : (i + 1) * LANES]
    if rest:
        side = LANES // rest
        short = rows // side
        at = at + whole * rows
        ref[at : at + short, :] = jnp.concatenate(
            [value[i * short : (i + 1) * short, whole * LANES :] for i in range(side)], axis=1
        )


def unpack(ref, at, rows, columns):
    whole, rest = columns // LANES, columns % LANES
    tiles = [ref[at + i * rows : at + (i + 1) * rows, :] for i in range(whole)]
    if rest:
        side = LANES // rest
        short = rows // side
        last = ref[at + whole * rows : at + whole * rows + short, :]
        tiles.append(
            jnp.concatenate([last[:, i * rest : (i + 1) * rest] for i in range(side)], axis=0)
        )
    return jnp.concatenate(tiles, axis=1)


def beside(parts, axis):
    cut = parts[0].shape[axis] // LANES * LANES
    size = parts[0].shape[axis]
    return jnp.concatenate(
        [lax.slice_in_dim(x, 0, cut, axis=axis) for x in parts]
        + [lax.slice_in_dim(x, cut, size, axis=axis) for x in parts],
        axis=axis,
    )


def embedded(img, txt, own, fixed, moving):
    core, _ = position()
    rows, span = img.shape
    a, b = img[...], txt[...]
    keep = jnp.where(core == 0, a, b) * RAISED
    travel = jnp.where(core == 0, b, a) * RAISED
    fixed[...] = keep
    moving[...] = travel
    pack(own, 0, keep)
    pack(own, packed_rows(rows, span), travel)


def pair_up(fixed, moving, got, pair):
    _, chip = position()
    rows, span = fixed.shape
    second = packed_rows(rows, span)
    for i, ref in enumerate((fixed, moving)):
        own, other = ref[...], unpack(got, i * second, rows, span)
        first, last = jnp.where(chip == 0, own, other), jnp.where(chip == 0, other, own)
        fill = jnp.zeros((rows, pair.shape[1] - 2 * span), F32)
        pair[i * rows : (i + 1) * rows, :] = jnp.concatenate(
            [beside([first, last], 1), fill], axis=1
        )


def widened(mine, theirs, span):
    cut = span // LANES * LANES
    middle, end = cut + span, 2 * span
    return jnp.concatenate(
        [mine[:, :cut], theirs[:, :cut], mine[:, cut : 2 * cut], theirs[:, cut : 2 * cut]]
        + [mine[:, 2 * cut : middle], theirs[:, 2 * cut : middle]]
        + [mine[:, middle:end], theirs[:, middle:end]],
        axis=1,
    )


def unit_rows(emb):
    inv = lax.rsqrt(jnp.sum(emb * emb, axis=1, keepdims=True) + 1e-06 * RAISED**2)
    return emb * inv, inv * RAISED


def wide_half(own, pair, peer, out):
    half = out.shape[0]
    rows = 2 * half
    _, chip = position()
    for first in (True, False):

        @pl.when((chip == 0) == (first == own))
        def _(first=first):
            at = 0 if first else half
            mine, theirs = pair[rows + at : rows + at + half, :], peer[at : at + half, :]
            unit, _ = unit_rows(widened(mine, theirs, out.shape[1] // 4))
            out[...] = unit.astype(BF16)


def relayed_half(pair, peer, other_half):
    wide_half(False, pair, peer, other_half)


def fixed_and_half(pair, peer, fixed, own_half, unit, inv):
    rows, width = fixed.shape
    wide = widened(pair[:rows, :], peer[rows:, :], width // 4)
    unit[...], inv[...] = unit_rows(wide)
    fixed[...] = unit[...].astype(BF16)
    wide_half(True, pair, peer, own_half)


def pull(factors, fixed, block, sign=None):
    logits = factors[0:1, 0:1] * lax.dot_general(
        fixed, block, BY_COLUMNS, preferred_element_type=F32
    ) + factors[1:2, 0:1]
    if sign is None:
        weight = 16.0 * jax.nn.sigmoid(logits)
    else:
        weight = -16.0 * sign * jax.nn.sigmoid(-sign * logits)
    return jnp.dot(weight.astype(BF16), block, preferred_element_type=F32)


def first_sum(factors, fixed, sign, own_half, *refs):
    a = fixed[...]
    block = jnp.concatenate([x[...] for x in refs[:-1]], axis=0)
    refs[-1][...] = pull(factors, a, own_half[...], sign[...]) + pull(factors, a, block)


def next_sum(factors, fixed, before, *refs):
    block = jnp.concatenate([x[...] for x in refs[:-1]], axis=0)
    refs[-1][...] = before[...] + pull(factors, fixed[...], block)


def last_sum(factors, fixed, before, far_opposite, unit, inv, keep, give):
    _, chip = position()
    rows, width = fixed.shape
    span = width // 4
    cut = span // LANES * LANES
    total = before[...] + pull(factors, fixed[...], far_opposite[...])
    inner = jnp.sum(unit[...] * total, axis=1, keepdims=True)
    across = (total - unit[...] * inner) * (factors[0:1, 0:1] * inv[...])
    middle = 4 * cut + 2 * (span - cut)
    first = jnp.concatenate([across[:, : 2 * cut], across[:, 4 * cut : middle]], axis=1)
    last = jnp.concatenate([across[:, 2 * cut : 4 * cut], across[:, middle:]], axis=1)
    keep[...] = jnp.where(chip == 0, first, last)
    pack(give, 0, jnp.where(chip == 0, last, first).astype(BF16))


def through_matrix(kept, got, mine, peer, to_chip, to_cross, to_core, keep, stacked):
    core, chip = position()
    rows, width = kept.shape
    span = width // 2
    demb = kept[...] + unpack(got, 0, rows, width).astype(F32)
    high = demb.astype(BF16)
    stacked[:rows, :] = high
    stacked[rows:, :] = (demb - high.astype(F32)).astype(BF16)
    matrix = beside([mine[...], peer[...]], 0)
    part = jnp.dot(stacked[...], matrix, preferred_element_type=F32)
    part = part[:rows] + part[rows:]
    spans = [part[:, u * span : (u + 1) * span] for u in range(4)]
    for t in range(4):

        @pl.when(2 * chip + core == t)
        def _(t=t):
            pack(to_chip, 0, spans[t ^ 2].astype(BF16))
            pack(to_cross, 0, spans[t ^ 3].astype(BF16))
            pack(to_core, 0, spans[t ^ 1].astype(BF16))
            keep[...] = spans[t]


def last_add(from_chip, from_cross, from_core, kept, img, txt):
    core, chip = position()
    rows, span = kept.shape
    core0 = core == 0
    mine = kept[...] + unpack(from_chip, 0, rows, span).astype(F32)
    theirs = unpack(from_core, 0, rows, span).astype(F32)
    theirs = theirs + unpack(from_cross, 0, rows, span).astype(F32)
    img[...] = jnp.where(core0, mine, theirs)
    txt[...] = jnp.where(core0, theirs, mine)


def shards(
    picture_averaged_vectors,
    picture_mapping_matrix,
    caption_averaged_vectors,
    caption_mapping_matrix,
    sharpness_factor,
    offset_term,
    paired_caption_index,
):
    groups = lax.axis_size("dp")
    rows = picture_averaged_vectors.shape[0]
    half = rows // 2
    span = picture_mapping_matrix.shape[1]
    width = 4 * span
    t = lax.axis_index("tensor")
    core0 = t % 2 == 0
    chip0 = t < 2
    factors = jnp.concatenate([sharpness_factor, offset_term])
    factors = jnp.broadcast_to(factors[:, None], (2, LANES))

    img_emb = jnp.dot(
        picture_averaged_vectors, picture_mapping_matrix, preferred_element_type=F32
    )
    txt_emb = jnp.dot(
        caption_averaged_vectors, caption_mapping_matrix, preferred_element_type=F32
    )
    emb_piece = ((rows, span), F32)
    own, fixed_own, moving_own = call(
        embedded,
        [((2 * packed_rows(rows, span), LANES), F32), emb_piece, emb_piece],
        img_emb,
        txt_emb,
    )
    sent = own.astype(F16)
    other = exchange(sent, groups, chip_swap).astype(F32)
    img_matrix, txt_matrix, _ = lax.optimization_barrier(
        (picture_mapping_matrix.T, caption_mapping_matrix.T, sent)
    )
    matrix_mine = jnp.where(core0, img_matrix, txt_matrix)
    matrix_theirs = jnp.where(core0, txt_matrix, img_matrix)
    matrix_peer = exchange(matrix_theirs, groups, core_swap)
    first_row = lax.axis_index("dp") * rows
    ids = first_row + jnp.arange(rows, dtype=jnp.int32)
    half_ids = jnp.where(chip0, ids[:half], ids[half:])
    half_index = jnp.where(chip0, paired_caption_index[:half], paired_caption_index[half:])
    matched = jnp.where(
        core0,
        paired_caption_index[:, None] == half_ids[None, :],
        ids[:, None] == half_index[None, :],
    )
    sign = jnp.where(matched, 1.0, -1.0).astype(F32)
    other, sign = lax.optimization_barrier((other, sign))
    pair_width = 2 * (span // LANES * LANES) + LANES
    (pair,) = call(pair_up, [((2 * rows, pair_width), F32)], fixed_own, moving_own, other)
    peer = exchange(pair.astype(F16), groups, core_swap)
    peer, matrix_peer = lax.optimization_barrier((peer, matrix_peer))
    peer = peer.astype(F32)
    half_width = ((half, width), BF16)
    (other_half,) = call(relayed_half, [half_width], pair, peer)
    pair, peer, other_half = lax.optimization_barrier((pair, peer, other_half))
    fixed, own_half, unit, inv = call(
        fixed_and_half,
        [((rows, width), BF16), half_width, ((rows, width), F32), ((rows, 1), F32)],
        pair,
        peer,
    )

    sums = [((rows, width), F32)]
    near_relayed = exchange(other_half, groups, neighbour)
    far_own = exchange(own_half, groups, beyond)
    near_other = exchange(own_half, groups, neighbour)
    opposite = exchange(near_relayed, groups, relay)
    (total,) = call(first_sum, sums, factors, fixed, sign, own_half, near_relayed)
    far_own, near_sent = lax.optimization_barrier((far_own, near_relayed))
    far_relayed = exchange(near_sent, groups, beyond)
    near_other, total = lax.optimization_barrier((near_other, total))
    far_other = exchange(near_other, groups, beyond)
    far_opposite = exchange(opposite, groups, beyond)
    (total,) = call(next_sum, sums, factors, fixed, total, far_own, near_other, opposite, far_relayed, far_other)
    keep, give = call(
        last_sum,
        [((rows, 2 * span), F32), ((packed_rows(rows, 2 * span), LANES), BF16)],
        factors,
        fixed,
        total,
        far_opposite,
        unit,
        inv,
    )
    got = exchange(give, groups, chip_swap)
    part = ((rows, span), F32)
    sent = ((packed_rows(rows, span), LANES), BF16)
    to_chip, to_cross, to_core, keep = call(
        through_matrix,
        [sent, sent, sent, part],
        keep,
        got,
        matrix_mine,
        matrix_peer,
        scratch=[((2 * rows, 2 * span), BF16)],
    )
    from_chip = exchange(to_chip, groups, chip_swap)
    from_cross = exchange(to_cross, groups, cross_swap)
    from_core = exchange(to_core, groups, core_swap)
    return tuple(call(last_add, [part, part], from_chip, from_cross, from_core, keep))


def solution(mesh):
    in_specs = (
        P("dp", None),
        P(None, "tensor"),
        P("dp", None),
        P(None, "tensor"),
        P(),
        P(),
        P("dp"),
    )
    out_specs = (P("dp", "tensor"), P("dp", "tensor"))
    return jax.shard_map(shards, mesh=mesh, in_specs=in_specs, out_specs=out_specs, check_vma=False)
```
